32 devices in a mesh: groups: 2 (over y), dp: 4 (over z), layer: 2 (over x), tensor: 2 (over core).
Axes of the slice: x: 2, y: 2, z: 4, core: 2. Of those that a mesh axis runs over, the one named last changes fastest.
Arguments:
- activations: bfloat16 [2, 1536, 14336], P('layer', ('groups', 'dp'), 'tensor'), parts along dimension 1, may hold values from -6 to 6
- out_grads: bfloat16 [2, 1536, 4096], P('layer', ('groups', 'dp'), 'tensor'), parts along dimension 1, may hold values from -6 to 6
- proj_in: bfloat16 [2, 64, 14336], P('layer', None, 'tensor'), may hold values from -0.046875 to 0.046875
- proj_out: bfloat16 [2, 64, 4096], P('layer', None, 'tensor'), may hold values from -0.09375 to 0.09375
- queries: bfloat16 [2, 256, 4096], P('layer', 'dp'), may hold values from -0.0068359375 to 0.0068359375
- lengths: int32 [16], P('groups'), parts along dimension 0, may hold values from 1 to 192, 768 in all
- owner_slot: int32 [16], P('groups'), parts along dimension 0, may hold values from 0 to 7, each once
- pad_mask: int32 [1536], P(('groups', 'dp')), parts along dimension 0, may hold values 0 or 1
Outputs:
- scores: float32 [16, 256], P(('groups', 'dp'), 'layer'), parts along dimension 0
The draws below stay inside these ranges and needn't reach their ends.
There are 2 independent parts, one for each index of `groups`. The reference program is written for one: setup_inputs(seed, part) draws one part's arguments, and reference() takes and returns one part's arrays. A program takes and returns all parts, laid end to end along the dimension named above; an argument that names none is the same for every part. Nothing has to cross between parts.
Inputs may be any that keep to these rules, and one draw needn't show every extreme that they name: `owner_slot`: every output row is the row of exactly one example. The lengths sum to 768; the longest example has exactly 192 tokens.
All inputs are finite; a program needn't handle non-finite values. No bound on the sum of `pad_mask` on one device may be relied on, other than what follows from the above.
Results may differ from the reference program's by a relative error of at most 0.0051.
Values may be sent and summed in bfloat16 or wider, within the bound.
A program may use at most 64 MiB of HBM per device.

```python
import math
import jax
import jax.numpy as jnp
import numpy as np
from jax import lax

D = 4096
FF = 14336
R_IN = 64
R_OUT = 64
SKETCH = 4096
QUERIES = 256
TOK_DEV = 192
LAYERS = 2
TOKENS = 768
EXAMPLES = 8
MAXLEN = 192


def plant(result, rng, smallest, top_value):
    spot = [jax.random.randint(jax.random.fold_in(rng, axis), (), 0, length) for axis, length in enumerate(result.shape)]
    longest = result.shape.index(max(result.shape))
    next_to = spot[:longest] + [(spot[longest] + 1) % result.shape[longest]] + spot[longest + 1:]
    return result.at[tuple(spot)].set(smallest).at[tuple(next_to)].set(top_value)


def block_levels(own_key, extent, cuts, low, top_value):
    level = 1.0
    for dim, parts in cuts:
        draws = jax.random.uniform(jax.random.fold_in(jax.random.fold_in(own_key, 6), dim), (parts,), jnp.float32, low / len(cuts), top_value / len(cuts))
        level = level * jnp.repeat(jnp.exp(draws), extent[dim] // parts).reshape((-1,) + (1,) * (len(extent) - 1 - dim))
    return level


def split_up(number_of, total, reach, skew):
    portions = [(1 << 20) // math.isqrt(rank ** skew) + 1 for rank in range(2, number_of + 1)]
    surplus, counts = total - reach - (number_of - 1), [1] * (number_of - 1)
    while surplus > 0:
        free = [i for i in range(number_of - 1) if counts[i] < reach]
        pool, budget = sum([portions[i] for i in free]), surplus
        for i in free:
            extra = min(reach - counts[i], max(1, budget * portions[i] // pool), surplus)
            counts[i] = counts[i] + extra
            surplus = surplus - extra
    return np.array([reach] + counts)


def ragged(rng, count, total, limit, skew):
    if count == 2:
        one = jax.random.randint(rng, (), max(1, total - limit), min(limit, total - 1) + 1)
        return jnp.stack([one, total - one])
    tallies = jnp.asarray(split_up(count, total, limit, skew), jnp.int32)
    pairs = (count - 1) // 2
    source_of, receiver = tallies[1:1 + 2 * pairs:2], tallies[2:2 + 2 * pairs:2]
    margin = jnp.minimum(source_of - 1, limit - receiver)
    shifted = jax.random.randint(jax.random.fold_in(rng, 1), (pairs,), 0, 1 << 20) % (margin + 1)
    tallies = tallies.at[1:1 + 2 * pairs:2].set(source_of - shifted).at[2:2 + 2 * pairs:2].set(receiver + shifted)
    return tallies[jax.random.permutation(jax.random.fold_in(rng, 2), count)]


def bell_draw(stream_key, dims, scale, limit, split=(), held_as=jnp.bfloat16):
    level = block_levels(stream_key, dims, split, -0.22, 0.18) if split else 1.0
    array = jax.random.normal(stream_key, dims, jnp.float32) * scale * level
    return jnp.minimum(jnp.maximum(array, -limit), limit).astype(held_as)


def setup_inputs(seed: int = 0, part: int = 0) -> dict:
    key_list = jax.random.split(jax.random.key(seed), 9)
    part_keys = jax.random.split(jax.random.fold_in(key_list[8], part), 9)
    return {
        "activations": bell_draw(part_keys[0], (LAYERS, TOKENS, FF), 1.0, 6.0, ((0, 2), (1, 4), (2, 2))),
        "out_grads": bell_draw(part_keys[1], (LAYERS, TOKENS, D), 1.0, 6.0, ((0, 2), (1, 4), (2, 2))),
        "proj_in": bell_draw(key_list[2], (LAYERS, R_IN, FF), FF ** -0.5, 0.046875, ((0, 2), (2, 2))),
        "proj_out": bell_draw(key_list[3], (LAYERS, R_OUT, D), D ** -0.5, 0.09375, ((0, 2), (2, 2))),
        "queries": bell_draw(key_list[4], (LAYERS, QUERIES, SKETCH), (LAYERS * SKETCH * TOK_DEV // 2) ** -0.5, 0.0068359375, ((0, 2), (1, 4))),
        "lengths": ragged(part_keys[5], EXAMPLES, TOKENS, MAXLEN, 2).astype(jnp.int32),
        "owner_slot": jax.random.permutation(part_keys[6], EXAMPLES).astype(jnp.int32),
        "pad_mask": plant((jax.random.randint(part_keys[7], (TOKENS,), 0, 4) < 3).astype(jnp.int32), jax.random.fold_in(part_keys[7], 1), 0, 1),
    }


def contract_last(left, right):
    return lax.dot_general(left, right, (((1,), (1,)), ((), ())), preferred_element_type=jnp.float32)


def reference(activations, out_grads, proj_in, proj_out, queries, lengths, owner_slot, pad_mask):
    example_ends = jnp.cumsum(lengths).astype(jnp.int32)
    positions = jnp.arange(TOKENS, dtype=jnp.int32)
    example_of = jnp.sum((positions[:, None] >= example_ends[None, :]).astype(jnp.int32), axis=1).astype(jnp.int32)
    slot_of = owner_slot[example_of]
    labels = jnp.arange(EXAMPLES, dtype=jnp.int32)
    member = jnp.where(slot_of[:, None] == labels[None, :], pad_mask[:, None], 0).astype(jnp.bfloat16)

    def layer_scores(operands):
        acts, grads, p_input, p_output, query_rows = operands
        act_side = contract_last(acts, p_input).astype(jnp.bfloat16)
        grad_side = contract_last(grads, p_output).astype(jnp.bfloat16)
        weighted = (member[:, :, None] * grad_side[:, None, :]).reshape(TOKENS, EXAMPLES * R_OUT)
        sketch = lax.dot_general(weighted, act_side, (((0,), (0,)), ((), ())), preferred_element_type=jnp.float32)
        sketch = sketch.reshape(EXAMPLES, SKETCH).astype(jnp.bfloat16)
        return contract_last(sketch, query_rows)

    per_layer = lax.map(layer_scores, (activations, out_grads, proj_in, proj_out, queries))
    return jnp.sum(per_layer, axis=0)
```

```python
import functools
import jax
import jax.numpy as jnp
from jax import lax
from jax.experimental import pallas as pl
from jax.experimental.pallas import tpu as pltpu
from jax.sharding import PartitionSpec as P

F32 = jnp.float32
BF16 = jnp.bfloat16
NT = (((1,), (1,)), ((), ()))
MESH = pl.DeviceIdType.MESH


def chunks_of(width, most):
    count = most
    while width % (count * 128):
        count -= 1
    return count


def kernel(
    sizes, acts_hbm, grads_hbm, pin_hbm, pout_hbm, query_hbm, len_hbm, own_hbm, pad_hbm, out_ref,
    acts, grads, pin, pout, query, len_s, own_s, pad,
    pair_out, pair_in, gath, gt_ref, acc, sk, sbuf, fin,
    load_sem, pair_send, pair_recv, dp_send, dp_recv, fin_send, fin_recv,
):
    n_dp, n_layer, n_core = sizes
    q, l, c = lax.axis_index("dp"), lax.axis_index("layer"), lax.axis_index("tensor")
    tok = acts.shape[0]
    part = tok // n_core
    r_in, r_out = pin.shape[0], pout.shape[0]
    examples = own_s.shape[0]
    rows, q_out = out_ref.shape
    q_blk = query.shape[0]
    ratio = q_out // q_blk
    ff_chunks = chunks_of(acts.shape[1], 2)
    ff_cut = acts.shape[1] // ff_chunks

    loads = []

    def load(src, dst):
        copy = pltpu.make_async_copy(src, dst, load_sem.at[len(loads)])
        copy.start()
        loads.append(copy)
        return copy

    def token_rows(cc):
        owner = lax.rem(c + cc, n_core)
        return pl.ds(pl.multiple_of(owner * part, part), part)

    order = list(range(1, n_core)) + [0]
    pout_load = load(pout_hbm.at[0], pout)
    side_loads = {}
    pin_loads = {}
    for place, cc in enumerate(order):
        here = token_rows(cc)
        side_loads[cc, "g"] = load(grads_hbm.at[0, here, :], grads.at[here, :])
        for k in range(ff_chunks):
            cols = pl.ds(k * ff_cut, ff_cut)
            if place == 0:
                pin_loads[k] = load(pin_hbm.at[0, :, cols], pin.at[:, cols])
            side_loads[cc, k] = load(acts_hbm.at[0, here, cols], acts.at[here, cols])
    len_load = load(len_hbm, len_s)
    own_load = load(own_hbm, own_s)
    pad_load = load(pad_hbm, pad)
    query_load = load(query_hbm.at[0], query)

    barrier = pltpu.get_barrier_semaphore()
    at_home = q // ratio == l
    for cc in range(1, n_core):
        pl.semaphore_signal(
            barrier, 1, device_id={"tensor": lax.rem(c + cc, n_core)}, device_id_type=MESH
        )
    for k in range(1, n_dp):
        pl.semaphore_signal(
            barrier, 1, device_id={"dp": lax.rem(q + k, n_dp)}, device_id_type=MESH
        )

    def source(rr, ll, cc):
        return (
            l * ratio + lax.rem(q + rr, ratio),
            lax.rem(l + ll, n_layer),
            lax.rem(c + cc, n_core),
        )

    def greet(rr, ll, cc):
        sq, sl, sc = source(rr, ll, cc)
        pl.semaphore_signal(
            barrier, 1, device_id={"dp": sq, "layer": sl, "tensor": sc}, device_id_type=MESH
        )

    for rr in range(ratio):
        for ll in range(n_layer):
            for cc in range(n_core):
                if rr == ll == cc == 0:
                    pl.when(jnp.logical_not(at_home))(functools.partial(greet, rr, ll, cc))
                else:
                    greet(rr, ll, cc)

    def project(cc):
        here = token_rows(cc)
        if cc == order[0]:
            pout_load.wait()
        side_loads[cc, "g"].wait()
        g = lax.dot_general(grads[here, :], pout[...], NT, preferred_element_type=F32)
        a = None
        for k in range(ff_chunks):
            cols = pl.ds(k * ff_cut, ff_cut)
            if cc == order[0]:
                pin_loads[k].wait()
            side_loads[cc, k].wait()
            term = lax.dot_general(acts[here, cols], pin[:, cols], NT, preferred_element_type=F32)
            a = term if a is None else a + term
        return jnp.concatenate([g, a], axis=1)

    pair_copies = []
    for cc in order[:-1]:
        pair_out[cc - 1] = project(cc)
        if cc == order[0]:
            everyone = n_core - 1 + n_dp - 1 + n_dp * n_core
            pl.semaphore_wait(barrier, everyone - at_home.astype(jnp.int32))
        copy = pltpu.make_async_remote_copy(
            src_ref=pair_out.at[cc - 1],
            dst_ref=pair_in.at[cc - 1],
            send_sem=pair_send.at[cc - 1],
            recv_sem=pair_recv.at[cc - 1],
            device_id={"tensor": lax.rem(c + cc, n_core)},
            device_id_type=MESH,
        )
        copy.start()
        pair_copies.append(copy)
    mine = project(0)

    pad_load.wait()
    wide = tok
    mark = (
        lax.broadcasted_iota(jnp.int32, (part, wide), 0) + c * part
        == lax.broadcasted_iota(jnp.int32, (part, wide), 1)
    )
    column = jnp.sum(
        jnp.where(mark, jnp.broadcast_to(pad[...], (part, wide)).astype(F32), 0.0),
        axis=1, keepdims=True,
    )
    lane = lax.broadcasted_iota(jnp.int32, (part, r_out + r_in), 1)
    keep = jnp.where(lane < r_out, column, 1.0)

    for copy in pair_copies:
        copy.wait_recv()
    for cc in range(1, n_core):
        mine = mine + pair_in[cc - 1]
    gath[q] = (mine * keep).astype(BF16)

    hops = sorted(range(1, n_dp), key=lambda k: (abs(k - n_dp / 2), k))
    dp_copies = {}
    for k in hops:
        dp_copies[k] = pltpu.make_async_remote_copy(
            src_ref=gath.at[q],
            dst_ref=gath.at[q],
            send_sem=dp_send.at[k - 1],
            recv_sem=dp_recv.at[k - 1],
            device_id={"dp": lax.rem(q + k, n_dp)},
            device_id_type=MESH,
        )
        dp_copies[k].start()

    len_load.wait()
    own_load.wait()
    bounds = []
    start = jnp.int32(0)
    for e in range(examples):
        end = start + len_s[e]
        bounds.append((start, end, own_s[e]))
        start = end
    label = lax.broadcasted_iota(jnp.int32, (examples, part), 0)
    step_lane = lax.broadcasted_iota(jnp.int32, (examples, part), 1)

    block = max(1, 512 // examples)
    block = min(block, r_out)

    def gather_block(src, first):
        position = step_lane + (src * tok + c * part)
        slot = jnp.full((examples, part), -1, jnp.int32)
        for low, high, owner in bounds:
            inside = (position >= low) & (position < high)
            slot = jnp.where(inside, owner, slot)
        member = jnp.where(slot == label, 1.0, 0.0).astype(F32)
        both = gath[src].astype(F32)
        gt_ref[...] = both.T[:r_out]
        side = both[:, r_out:]
        reps = 128 // r_in
        side = jnp.concatenate([side] * reps, axis=1).astype(BF16)
        for b in range(r_out // block):
            weighted = jnp.concatenate(
                [
                    jnp.broadcast_to(gt_ref[pl.ds(b * block + i, 1), :], (examples, part)) * member
                    for i in range(block)
                ],
                axis=0,
            ).astype(BF16)
            term = jnp.dot(weighted, side, preferred_element_type=F32)
            where = pl.ds(b * block * examples, block * examples)
            if first:
                acc[where, :] = term
            else:
                acc[where, :] += term

    gather_block(q, True)
    for k in hops:
        dp_copies[k].wait_recv()
        gather_block(lax.rem(q + n_dp - k, n_dp), False)

    reps = 128 // r_in
    lanes = lax.broadcasted_iota(jnp.int32, (examples, 128), 1) // r_in
    for t in range(r_out // reps):
        tile = acc[pl.ds(t * reps * examples, examples), :]
        for j in range(1, reps):
            other = acc[pl.ds((t * reps + j) * examples, examples), :]
            tile = jnp.where(lanes == j, other, tile)
        sk[:, pl.ds(t * 128, 128)] = tile.astype(BF16)

    query_load.wait()
    scores = lax.dot_general(sk[...], query[...], NT, preferred_element_type=F32)
    spread = jnp.concatenate([scores] * ratio, axis=1)
    spot = lax.broadcasted_iota(jnp.int32, (examples, q_out), 1) // q_blk
    spread = jnp.where(spot == lax.rem(q, ratio), spread, 0.0)
    for d in range(n_dp):
        sbuf[d] = spread[d * rows:(d + 1) * rows]

    def slot_at(sq, sl, sc):
        return (lax.rem(sq, ratio) * n_layer + sl) * n_core + sc

    my_slot = slot_at(q, l, c)

    def final_copy(dd, cc):
        d = lax.rem(q + dd, n_dp)
        return pltpu.make_async_remote_copy(
            src_ref=sbuf.at[d],
            dst_ref=fin.at[my_slot],
            send_sem=fin_send.at[dd * n_core + cc],
            recv_sem=fin_recv.at[my_slot],
            device_id={"dp": d, "layer": q // ratio, "tensor": lax.rem(c + cc, n_core)},
            device_id_type=MESH,
        )

    for dd in range(n_dp):
        for cc in range(n_core):
            if dd == cc == 0:
                @pl.when(at_home)
                def _():
                    fin[my_slot] = sbuf[q]

                @pl.when(jnp.logical_not(at_home))
                def _():
                    final_copy(0, 0).start()
            else:
                final_copy(dd, cc).start()

    def arrived(rr, ll, cc):
        slot = slot_at(*source(rr, ll, cc))
        pltpu.make_async_remote_copy(
            src_ref=sbuf.at[0],
            dst_ref=fin.at[slot],
            send_sem=fin_send.at[0],
            recv_sem=fin_recv.at[slot],
            device_id={"tensor": lax.rem(c + 1, n_core)},
            device_id_type=MESH,
        ).wait_recv()

    for rr in range(ratio):
        for ll in range(n_layer):
            for cc in range(n_core):
                if rr == ll == cc == 0:
                    pl.when(jnp.logical_not(at_home))(functools.partial(arrived, rr, ll, cc))
                else:
                    arrived(rr, ll, cc)
    total = fin[0]
    for s in range(1, fin.shape[0]):
        total = total + fin[s]
    out_ref[...] = total

    for copy in pair_copies:
        copy.wait_send()
    for k in hops:
        dp_copies[k].wait_send()
    for dd in range(n_dp):
        for cc in range(n_core):
            if dd == cc == 0:
                @pl.when(jnp.logical_not(at_home))
                def _():
                    final_copy(0, 0).wait_send()
            else:
                final_copy(dd, cc).wait_send()


def local(sizes, activations, out_grads, proj_in, proj_out, queries, lengths, owner_slot, pad_mask):
    n_dp, n_layer, n_core = sizes
    tok = activations.shape[1]
    part = tok // n_core
    r_in, r_out = proj_in.shape[1], proj_out.shape[1]
    examples = lengths.shape[0]
    rows = examples // n_dp
    q_blk = queries.shape[1]
    q_out = q_blk * n_dp // n_layer
    sources = n_dp * n_core
    any_spec = pl.BlockSpec(memory_space=pltpu.HBM)
    return pl.pallas_call(
        functools.partial(kernel, sizes),
        out_shape=jax.ShapeDtypeStruct((rows, q_out), F32),
        in_specs=[any_spec] * 8,
        out_specs=pl.BlockSpec(memory_space=pltpu.VMEM),
        scratch_shapes=[
            pltpu.VMEM(activations.shape[1:], BF16),
            pltpu.VMEM(out_grads.shape[1:], BF16),
            pltpu.VMEM(proj_in.shape[1:], BF16),
            pltpu.VMEM(proj_out.shape[1:], BF16),
            pltpu.VMEM(queries.shape[1:], BF16),
            pltpu.SMEM((examples,), jnp.int32),
            pltpu.SMEM((examples,), jnp.int32),
            pltpu.VMEM((1, tok), jnp.int32),
            pltpu.VMEM((n_core - 1, part, r_out + r_in), F32),
            pltpu.VMEM((n_core - 1, part, r_out + r_in), F32),
            pltpu.VMEM((n_dp, part, r_out + r_in), BF16),
            pltpu.VMEM((r_out, part), F32),
            pltpu.VMEM((r_out * examples, 128), F32),
            pltpu.VMEM((examples, r_out * r_in), BF16),
            pltpu.VMEM((n_dp, rows, q_out), F32),
            pltpu.VMEM((sources, rows, q_out), F32),
            pltpu.SemaphoreType.DMA((32,)),
            pltpu.SemaphoreType.DMA((n_core - 1,)),
            pltpu.SemaphoreType.DMA((n_core - 1,)),
            pltpu.SemaphoreType.DMA((n_dp - 1,)),
            pltpu.SemaphoreType.DMA((n_dp - 1,)),
            pltpu.SemaphoreType.DMA((sources,)),
            pltpu.SemaphoreType.DMA((sources,)),
        ],
        compiler_params=pltpu.CompilerParams(
            collective_id=0, has_side_effects=True, vmem_limit_bytes=63 * 1024 * 1024
        ),
    )(
        activations, out_grads, proj_in, proj_out, queries, lengths, owner_slot,
        pad_mask.reshape(1, tok),
    )


def solution(mesh):
    sizes = (mesh.shape["dp"], mesh.shape["layer"], mesh.shape["tensor"])
    placed = (
        P("layer", ("groups", "dp"), "tensor"),
        P("layer", ("groups", "dp"), "tensor"),
        P("layer", None, "tensor"),
        P("layer", None, "tensor"),
        P("layer", "dp", None),
        P("groups"),
        P("groups"),
        P(("groups", "dp")),
    )
    return jax.shard_map(
        functools.partial(local, sizes), mesh=mesh, in_specs=placed,
        out_specs=P(("groups", "dp"), "layer"), check_vma=False,
    )
```

```python
import functools
import jax
import jax.numpy as jnp
from jax import lax
from jax.experimental import pallas as pl
from jax.experimental.pallas import tpu as pltpu
from jax.sharding import PartitionSpec as P

F32 = jnp.float32
BF16 = jnp.bfloat16
NT = (((1,), (1,)), ((), ()))
MESH = pl.DeviceIdType.MESH


def chunks_of(width, most):
    count = most
    while width % (count * 128):
        count -= 1
    return count


def kernel(
    sizes, acts_hbm, grads_hbm, pin_hbm, pout_hbm, query_hbm, len_hbm, own_hbm, pad_hbm, out_ref,
    acts, grads, pin, pout, query, len_s, own_s, pad,
    pair_out, pair_in, gath, gt_ref, acc, sk, sbuf, fin,
    load_sem, pair_send, pair_recv, dp_send, dp_recv, fin_send, fin_recv,
):
    n_dp, n_layer, n_core = sizes
    q, l, c = lax.axis_index("dp"), lax.axis_index("layer"), lax.axis_index("tensor")
    tok = acts.shape[0]
    part = tok // n_core
    r_in, r_out = pin.shape[0], pout.shape[0]
    examples = own_s.shape[0]
    rows, q_out = out_ref.shape
    q_blk = query.shape[0]
    ratio = q_out // q_blk
    ff_chunks = chunks_of(acts.shape[1], 2)
    ff_cut = acts.shape[1] // ff_chunks

    barrier = pltpu.get_barrier_semaphore()
    at_home = q // ratio == l
    for cc in range(1, n_core):
        pl.semaphore_signal(
            barrier, 1, device_id={"tensor": lax.rem(c + cc, n_core)}, device_id_type=MESH
        )
    for k in range(1, n_dp):
        pl.semaphore_signal(
            barrier, 1, device_id={"dp": lax.rem(q + k, n_dp)}, device_id_type=MESH
        )

    def source(rr, ll, cc):
        return (
            l * ratio + lax.rem(q + rr, ratio),
            lax.rem(l + ll, n_layer),
            lax.rem(c + cc, n_core),
        )

    def greet(rr, ll, cc):
        sq, sl, sc = source(rr, ll, cc)
        pl.semaphore_signal(
            barrier, 1, device_id={"dp": sq, "layer": sl, "tensor": sc}, device_id_type=MESH
        )

    for rr in range(ratio):
        for ll in range(n_layer):
            for cc in range(n_core):
                if rr == ll == cc == 0:
                    pl.when(jnp.logical_not(at_home))(functools.partial(greet, rr, ll, cc))
                else:
                    greet(rr, ll, cc)

    loads = []

    def load(src, dst):
        copy = pltpu.make_async_copy(src, dst, load_sem.at[len(loads)])
        copy.start()
        loads.append(copy)
        return copy

    def token_rows(cc):
        owner = lax.rem(c + cc, n_core)
        return pl.ds(pl.multiple_of(owner * part, part), part)

    order = list(range(1, n_core)) + [0]
    pout_load = load(pout_hbm.at[0], pout)
    side_loads = {}
    pin_loads = {}
    for place, cc in enumerate(order):
        here = token_rows(cc)
        side_loads[cc, "g"] = load(grads_hbm.at[0, here, :], grads.at[here, :])
        for k in range(ff_chunks):
            cols = pl.ds(k * ff_cut, ff_cut)
            if place == 0:
                pin_loads[k] = load(pin_hbm.at[0, :, cols], pin.at[:, cols])
            side_loads[cc, k] = load(acts_hbm.at[0, here, cols], acts.at[here, cols])
    len_load = load(len_hbm, len_s)
    own_load = load(own_hbm, own_s)
    pad_load = load(pad_hbm, pad)
    query_load = load(query_hbm.at[0], query)

    def project(cc):
        here = token_rows(cc)
        if cc == order[0]:
            pout_load.wait()
        side_loads[cc, "g"].wait()
        g = lax.dot_general(grads[here, :], pout[...], NT, preferred_element_type=F32)
        a = None
        for k in range(ff_chunks):
            cols = pl.ds(k * ff_cut, ff_cut)
            if cc == order[0]:
                pin_loads[k].wait()
            side_loads[cc, k].wait()
            term = lax.dot_general(acts[here, cols], pin[:, cols], NT, preferred_element_type=F32)
            a = term if a is None else a + term
        return jnp.concatenate([g, a], axis=1)

    pair_copies = []
    for cc in order[:-1]:
        pair_out[cc - 1] = project(cc)
        if cc == order[0]:
            everyone = n_core - 1 + n_dp - 1 + n_dp * n_core
            pl.semaphore_wait(barrier, everyone - at_home.astype(jnp.int32))
        copy = pltpu.make_async_remote_copy(
            src_ref=pair_out.at[cc - 1],
            dst_ref=pair_in.at[cc - 1],
            send_sem=pair_send.at[cc - 1],
            recv_sem=pair_recv.at[cc - 1],
            device_id={"tensor": lax.rem(c + cc, n_core)},
            device_id_type=MESH,
        )
        copy.start()
        pair_copies.append(copy)
    mine = project(0)

    pad_load.wait()
    wide = tok
    mark = (
        lax.broadcasted_iota(jnp.int32, (part, wide), 0) + c * part
        == lax.broadcasted_iota(jnp.int32, (part, wide), 1)
    )
    column = jnp.sum(
        jnp.where(mark, jnp.broadcast_to(pad[...], (part, wide)).astype(F32), 0.0),
        axis=1, keepdims=True,
    )
    lane = lax.broadcasted_iota(jnp.int32, (part, r_out + r_in), 1)
    keep = jnp.where(lane < r_out, column, 1.0)

    for copy in pair_copies:
        copy.wait_recv()
    for cc in range(1, n_core):
        mine = mine + pair_in[cc - 1]
    gath[q] = (mine * keep).astype(BF16)

    hops = sorted(range(1, n_dp), key=lambda k: (abs(k - n_dp / 2), k))
    dp_copies = {}
    for k in hops:
        dp_copies[k] = pltpu.make_async_remote_copy(
            src_ref=gath.at[q],
            dst_ref=gath.at[q],
            send_sem=dp_send.at[k - 1],
            recv_sem=dp_recv.at[k - 1],
            device_id={"dp": lax.rem(q + k, n_dp)},
            device_id_type=MESH,
        )
        dp_copies[k].start()

    len_load.wait()
    own_load.wait()
    bounds = []
    start = jnp.int32(0)
    for e in range(examples):
        end = start + len_s[e]
        bounds.append((start, end, own_s[e]))
        start = end
    label = lax.broadcasted_iota(jnp.int32, (examples, part), 0)
    step_lane = lax.broadcasted_iota(jnp.int32, (examples, part), 1)

    block = max(1, 512 // examples)
    block = min(block, r_out)

    def gather_block(src, first):
        position = step_lane + (src * tok + c * part)
        slot = jnp.full((examples, part), -1, jnp.int32)
        for low, high, owner in bounds:
            inside = (position >= low) & (position < high)
            slot = jnp.where(inside, owner, slot)
        member = jnp.where(slot == label, 1.0, 0.0).astype(F32)
        both = gath[src].astype(F32)
        gt_ref[...] = both.T[:r_out]
        side = both[:, r_out:]
        reps = 128 // r_in
        side = jnp.concatenate([side] * reps, axis=1).astype(BF16)
        for b in range(r_out // block):
            weighted = jnp.concatenate(
                [
                    jnp.broadcast_to(gt_ref[pl.ds(b * block + i, 1), :], (examples, part)) * member
                    for i in range(block)
                ],
                axis=0,
            ).astype(BF16)
            term = jnp.dot(weighted, side, preferred_element_type=F32)
            where = pl.ds(b * block * examples, block * examples)
            if first:
                acc[where, :] = term
            else:
                acc[where, :] += term

    gather_block(q, True)
    for k in hops:
        dp_copies[k].wait_recv()
        gather_block(lax.rem(q + n_dp - k, n_dp), False)

    reps = 128 // r_in
    lanes = lax.broadcasted_iota(jnp.int32, (examples, 128), 1) // r_in
    for t in range(r_out // reps):
        tile = acc[pl.ds(t * reps * examples, examples), :]
        for j in range(1, reps):
            other = acc[pl.ds((t * reps + j) * examples, examples), :]
            tile = jnp.where(lanes == j, other, tile)
        sk[:, pl.ds(t * 128, 128)] = tile.astype(BF16)

    query_load.wait()
    scores = lax.dot_general(sk[...], query[...], NT, preferred_element_type=F32)
    spread = jnp.concatenate([scores] * ratio, axis=1)
    spot = lax.broadcasted_iota(jnp.int32, (examples, q_out), 1) // q_blk
    spread = jnp.where(spot == lax.rem(q, ratio), spread, 0.0)
    for d in range(n_dp):
        sbuf[d] = spread[d * rows:(d + 1) * rows]

    def slot_at(sq, sl, sc):
        return (lax.rem(sq, ratio) * n_layer + sl) * n_core + sc

    my_slot = slot_at(q, l, c)

    def final_copy(dd, cc):
        d = lax.rem(q + dd, n_dp)
        return pltpu.make_async_remote_copy(
            src_ref=sbuf.at[d],
            dst_ref=fin.at[my_slot],
            send_sem=fin_send.at[dd * n_core + cc],
            recv_sem=fin_recv.at[my_slot],
            device_id={"dp": d, "layer": q // ratio, "tensor": lax.rem(c + cc, n_core)},
            device_id_type=MESH,
        )

    for dd in range(n_dp):
        for cc in range(n_core):
            if dd == cc == 0:
                @pl.when(at_home)
                def _():
                    fin[my_slot] = sbuf[q]

                @pl.when(jnp.logical_not(at_home))
                def _():
                    final_copy(0, 0).start()
            else:
                final_copy(dd, cc).start()

    def arrived(rr, ll, cc):
        slot = slot_at(*source(rr, ll, cc))
        pltpu.make_async_remote_copy(
            src_ref=sbuf.at[0],
            dst_ref=fin.at[slot],
            send_sem=fin_send.at[0],
            recv_sem=fin_recv.at[slot],
            device_id={"tensor": lax.rem(c + 1, n_core)},
            device_id_type=MESH,
        ).wait_recv()

    for rr in range(ratio):
        for ll in range(n_layer):
            for cc in range(n_core):
                if rr == ll == cc == 0:
                    pl.when(jnp.logical_not(at_home))(functools.partial(arrived, rr, ll, cc))
                else:
                    arrived(rr, ll, cc)
    total = fin[0]
    for s in range(1, fin.shape[0]):
        total = total + fin[s]
    out_ref[...] = total

    for copy in pair_copies:
        copy.wait_send()
    for k in hops:
        dp_copies[k].wait_send()
    for dd in range(n_dp):
        for cc in range(n_core):
            if dd == cc == 0:
                @pl.when(jnp.logical_not(at_home))
                def _():
                    final_copy(0, 0).wait_send()
            else:
                final_copy(dd, cc).wait_send()


def local(sizes, activations, out_grads, proj_in, proj_out, queries, lengths, owner_slot, pad_mask):
    n_dp, n_layer, n_core = sizes
    tok = activations.shape[1]
    part = tok // n_core
    r_in, r_out = proj_in.shape[1], proj_out.shape[1]
    examples = lengths.shape[0]
    rows = examples // n_dp
    q_blk = queries.shape[1]
    q_out = q_blk * n_dp // n_layer
    sources = n_dp * n_core
    any_spec = pl.BlockSpec(memory_space=pltpu.HBM)
    return pl.pallas_call(
        functools.partial(kernel, sizes),
        out_shape=pltpu.VMEM((rows, q_out), F32),
        in_specs=[any_spec] * 8,
        out_specs=pl.BlockSpec(memory_space=pltpu.VMEM),
        scratch_shapes=[
            pltpu.VMEM(activations.shape[1:], BF16),
            pltpu.VMEM(out_grads.shape[1:], BF16),
            pltpu.VMEM(proj_in.shape[1:], BF16),
            pltpu.VMEM(proj_out.shape[1:], BF16),
            pltpu.VMEM(queries.shape[1:], BF16),
            pltpu.SMEM((examples,), jnp.int32),
            pltpu.SMEM((examples,), jnp.int32),
            pltpu.VMEM((1, tok), jnp.int32),
            pltpu.VMEM((n_core - 1, part, r_out + r_in), F32),
            pltpu.VMEM((n_core - 1, part, r_out + r_in), F32),
            pltpu.VMEM((n_dp, part, r_out + r_in), BF16),
            pltpu.VMEM((r_out, part), F32),
            pltpu.VMEM((r_out * examples, 128), F32),
            pltpu.VMEM((examples, r_out * r_in), BF16),
            pltpu.VMEM((n_dp, rows, q_out), F32),
            pltpu.VMEM((sources, rows, q_out), F32),
            pltpu.SemaphoreType.DMA((32,)),
            pltpu.SemaphoreType.DMA((n_core - 1,)),
            pltpu.SemaphoreType.DMA((n_core - 1,)),
            pltpu.SemaphoreType.DMA((n_dp - 1,)),
            pltpu.SemaphoreType.DMA((n_dp - 1,)),
            pltpu.SemaphoreType.DMA((sources,)),
            pltpu.SemaphoreType.DMA((sources,)),
        ],
        compiler_params=pltpu.CompilerParams(
            collective_id=0, has_side_effects=True, vmem_limit_bytes=63 * 1024 * 1024
        ),
    )(
        activations, out_grads, proj_in, proj_out, queries, lengths, owner_slot,
        pad_mask.reshape(1, tok),
    )


def solution(mesh):
    sizes = (mesh.shape["dp"], mesh.shape["layer"], mesh.shape["tensor"])
    placed = (
        P("layer", ("groups", "dp"), "tensor"),
        P("layer", ("groups", "dp"), "tensor"),
        P("layer", None, "tensor"),
        P("layer", None, "tensor"),
        P("layer", "dp", None),
        P("groups"),
        P("groups"),
        P(("groups", "dp")),
    )
    return jax.shard_map(
        functools.partial(local, sizes), mesh=mesh, in_specs=placed,
        out_specs=P(("groups", "dp"), "layer"), check_vma=False,
    )
```

```python
import functools
import jax
import jax.numpy as jnp
from jax import lax
from jax.experimental import pallas as pl
from jax.experimental.pallas import tpu as pltpu
from jax.sharding import PartitionSpec as P

F32 = jnp.float32
BF16 = jnp.bfloat16
NT = (((1,), (1,)), ((), ()))
MESH = pl.DeviceIdType.MESH


def chunks_of(width, most):
    count = most
    while width % (count * 128):
        count -= 1
    return count


def kernel(
    sizes, acts_hbm, grads_hbm, pin_hbm, pout_hbm, query_hbm, len_hbm, own_hbm, pad_hbm, out_ref,
    acts, grads, pin, pout, query, len_s, own_s, pad,
    pair_out, pair_in, gath, gt_ref, acc, sk, sbuf, fin,
    load_sem, pair_send, pair_recv, dp_send, dp_recv, fin_send, fin_recv,
):
    n_dp, n_layer, n_core = sizes
    q, l, c = lax.axis_index("dp"), lax.axis_index("layer"), lax.axis_index("tensor")
    tok = acts.shape[0]
    part = tok // n_core
    r_in, r_out = pin.shape[0], pout.shape[0]
    examples = own_s.shape[0]
    rows, q_out = out_ref.shape
    q_blk = query.shape[0]
    ratio = q_out // q_blk
    ff_chunks = chunks_of(acts.shape[1], 4)
    ff_cut = acts.shape[1] // ff_chunks

    barrier = pltpu.get_barrier_semaphore()
    at_home = q // ratio == l
    for cc in range(1, n_core):
        pl.semaphore_signal(
            barrier, 1, device_id={"tensor": lax.rem(c + cc, n_core)}, device_id_type=MESH
        )
    for k in range(1, n_dp):
        pl.semaphore_signal(
            barrier, 1, device_id={"dp": lax.rem(q + k, n_dp)}, device_id_type=MESH
        )

    def source(rr, ll, cc):
        return (
            l * ratio + lax.rem(q + rr, ratio),
            lax.rem(l + ll, n_layer),
            lax.rem(c + cc, n_core),
        )

    def greet(rr, ll, cc):
        sq, sl, sc = source(rr, ll, cc)
        pl.semaphore_signal(
            barrier, 1, device_id={"dp": sq, "layer": sl, "tensor": sc}, device_id_type=MESH
        )

    for rr in range(ratio):
        for ll in range(n_layer):
            for cc in range(n_core):
                if rr == ll == cc == 0:
                    pl.when(jnp.logical_not(at_home))(functools.partial(greet, rr, ll, cc))
                else:
                    greet(rr, ll, cc)

    loads = []

    def load(src, dst):
        copy = pltpu.make_async_copy(src, dst, load_sem.at[len(loads)])
        copy.start()
        loads.append(copy)
        return copy

    def token_rows(cc):
        owner = lax.rem(c + cc, n_core)
        return pl.ds(pl.multiple_of(owner * part, part), part)

    order = list(range(1, n_core)) + [0]
    len_load = load(len_hbm, len_s)
    own_load = load(own_hbm, own_s)
    pad_load = load(pad_hbm, pad)
    pout_load = load(pout_hbm.at[0], pout)
    side_loads = {}
    pin_loads = {}
    for place, cc in enumerate(order):
        here = token_rows(cc)
        side_loads[cc, "g"] = load(grads_hbm.at[0, here, :], grads.at[here, :])
        for k in range(ff_chunks):
            cols = pl.ds(k * ff_cut, ff_cut)
            if place == 0:
                pin_loads[k] = load(pin_hbm.at[0, :, cols], pin.at[:, cols])
            side_loads[cc, k] = load(acts_hbm.at[0, here, cols], acts.at[here, cols])
    query_load = load(query_hbm.at[0], query)

    def project(cc):
        here = token_rows(cc)
        if cc == order[0]:
            pout_load.wait()
        side_loads[cc, "g"].wait()
        g = lax.dot_general(grads[here, :], pout[...], NT, preferred_element_type=F32)
        a = None
        for k in range(ff_chunks):
            cols = pl.ds(k * ff_cut, ff_cut)
            if cc == order[0]:
                pin_loads[k].wait()
            side_loads[cc, k].wait()
            term = lax.dot_general(acts[here, cols], pin[:, cols], NT, preferred_element_type=F32)
            a = term if a is None else a + term
        return jnp.concatenate([g, a], axis=1)

    pad_load.wait()
    wide = tok
    mark = (
        lax.broadcasted_iota(jnp.int32, (part, wide), 0) + c * part
        == lax.broadcasted_iota(jnp.int32, (part, wide), 1)
    )
    column = jnp.sum(
        jnp.where(mark, jnp.broadcast_to(pad[...], (part, wide)).astype(F32), 0.0),
        axis=1, keepdims=True,
    )
    lane = lax.broadcasted_iota(jnp.int32, (part, r_out + r_in), 1)
    keep = jnp.where(lane < r_out, column, 1.0)

    pair_copies = []
    for cc in order[:-1]:
        pair_out[cc - 1] = project(cc)
        if cc == order[0]:
            everyone = n_core - 1 + n_dp - 1 + n_dp * n_core
            pl.semaphore_wait(barrier, everyone - at_home.astype(jnp.int32))
        copy = pltpu.make_async_remote_copy(
            src_ref=pair_out.at[cc - 1],
            dst_ref=pair_in.at[cc - 1],
            send_sem=pair_send.at[cc - 1],
            recv_sem=pair_recv.at[cc - 1],
            device_id={"tensor": lax.rem(c + cc, n_core)},
            device_id_type=MESH,
        )
        copy.start()
        pair_copies.append(copy)
    mine = project(0)

    for copy in pair_copies:
        copy.wait_recv()
    for cc in range(1, n_core):
        mine = mine + pair_in[cc - 1]
    gath[q] = (mine * keep).astype(BF16)

    hops = sorted(range(1, n_dp), key=lambda k: (abs(k - n_dp / 2), k))
    dp_copies = {}
    for k in hops:
        dp_copies[k] = pltpu.make_async_remote_copy(
            src_ref=gath.at[q],
            dst_ref=gath.at[q],
            send_sem=dp_send.at[k - 1],
            recv_sem=dp_recv.at[k - 1],
            device_id={"dp": lax.rem(q + k, n_dp)},
            device_id_type=MESH,
        )
        dp_copies[k].start()

    len_load.wait()
    own_load.wait()
    bounds = []
    start = jnp.int32(0)
    for e in range(examples):
        end = start + len_s[e]
        bounds.append((start, end, own_s[e]))
        start = end
    label = lax.broadcasted_iota(jnp.int32, (examples, part), 0)
    step_lane = lax.broadcasted_iota(jnp.int32, (examples, part), 1)

    block = max(1, 512 // examples)
    block = min(block, r_out)

    def gather_block(src, first):
        position = step_lane + (src * tok + c * part)
        slot = jnp.full((examples, part), -1, jnp.int32)
        for low, high, owner in bounds:
            inside = (position >= low) & (position < high)
            slot = jnp.where(inside, owner, slot)
        member = jnp.where(slot == label, 1.0, 0.0).astype(F32)
        both = gath[src].astype(F32)
        gt_ref[...] = both.T[:r_out]
        side = both[:, r_out:]
        reps = 128 // r_in
        side = jnp.concatenate([side] * reps, axis=1).astype(BF16)
        for b in range(r_out // block):
            weighted = jnp.concatenate(
                [
                    jnp.broadcast_to(gt_ref[pl.ds(b * block + i, 1), :], (examples, part)) * member
                    for i in range(block)
                ],
                axis=0,
            ).astype(BF16)
            term = jnp.dot(weighted, side, preferred_element_type=F32)
            where = pl.ds(b * block * examples, block * examples)
            if first:
                acc[where, :] = term
            else:
                acc[where, :] += term

    gather_block(q, True)
    for k in hops:
        dp_copies[k].wait_recv()
        gather_block(lax.rem(q + n_dp - k, n_dp), False)

    reps = 128 // r_in
    lanes = lax.broadcasted_iota(jnp.int32, (examples, 128), 1) // r_in
    for t in range(r_out // reps):
        tile = acc[pl.ds(t * reps * examples, examples), :]
        for j in range(1, reps):
            other = acc[pl.ds((t * reps + j) * examples, examples), :]
            tile = jnp.where(lanes == j, other, tile)
        sk[:, pl.ds(t * 128, 128)] = tile.astype(BF16)

    query_load.wait()
    scores = lax.dot_general(sk[...], query[...], NT, preferred_element_type=F32)
    spread = jnp.concatenate([scores] * ratio, axis=1)
    spot = lax.broadcasted_iota(jnp.int32, (examples, q_out), 1) // q_blk
    spread = jnp.where(spot == lax.rem(q, ratio), spread, 0.0)
    for d in range(n_dp):
        sbuf[d] = spread[d * rows:(d + 1) * rows]

    def slot_at(sq, sl, sc):
        return (lax.rem(sq, ratio) * n_layer + sl) * n_core + sc

    my_slot = slot_at(q, l, c)

    def far_first(j):
        down = n_dp - 1 - j
        down = jnp.where(down <= q, down - 1, down)
        up = jnp.where(j >= q, j + 1, j)
        return jnp.where(q < n_dp // 2, down, up)

    def final_copy(dd, cc):
        d = q if dd == 0 else far_first(dd - 1)
        return pltpu.make_async_remote_copy(
            src_ref=sbuf.at[d],
            dst_ref=fin.at[my_slot],
            send_sem=fin_send.at[dd * n_core + cc],
            recv_sem=fin_recv.at[my_slot],
            device_id={"dp": d, "layer": q // ratio, "tensor": lax.rem(c + cc, n_core)},
            device_id_type=MESH,
        )

    for dd in list(range(1, n_dp)) + [0]:
        for cc in range(n_core):
            if dd == cc == 0:
                @pl.when(at_home)
                def _():
                    fin[my_slot] = sbuf[q]

                @pl.when(jnp.logical_not(at_home))
                def _():
                    final_copy(0, 0).start()
            else:
                final_copy(dd, cc).start()

    def arrived(rr, ll, cc):
        slot = slot_at(*source(rr, ll, cc))
        pltpu.make_async_remote_copy(
            src_ref=sbuf.at[0],
            dst_ref=fin.at[slot],
            send_sem=fin_send.at[0],
            recv_sem=fin_recv.at[slot],
            device_id={"tensor": lax.rem(c + 1, n_core)},
            device_id_type=MESH,
        ).wait_recv()

    for rr in range(ratio):
        for ll in range(n_layer):
            for cc in range(n_core):
                if rr == ll == cc == 0:
                    pl.when(jnp.logical_not(at_home))(functools.partial(arrived, rr, ll, cc))
                else:
                    arrived(rr, ll, cc)
    total = fin[0]
    for s in range(1, fin.shape[0]):
        total = total + fin[s]
    out_ref[...] = total

    for copy in pair_copies:
        copy.wait_send()
    for k in hops:
        dp_copies[k].wait_send()
    for dd in range(n_dp):
        for cc in range(n_core):
            if dd == cc == 0:
                @pl.when(jnp.logical_not(at_home))
                def _():
                    final_copy(0, 0).wait_send()
            else:
                final_copy(dd, cc).wait_send()


def local(sizes, activations, out_grads, proj_in, proj_out, queries, lengths, owner_slot, pad_mask):
    n_dp, n_layer, n_core = sizes
    tok = activations.shape[1]
    part = tok // n_core
    r_in, r_out = proj_in.shape[1], proj_out.shape[1]
    examples = lengths.shape[0]
    rows = examples // n_dp
    q_blk = queries.shape[1]
    q_out = q_blk * n_dp // n_layer
    sources = n_dp * n_core
    any_spec = pl.BlockSpec(memory_space=pltpu.HBM)
    return pl.pallas_call(
        functools.partial(kernel, sizes),
        out_shape=pltpu.VMEM((rows, q_out), F32),
        in_specs=[any_spec] * 8,
        out_specs=pl.BlockSpec(memory_space=pltpu.VMEM),
        scratch_shapes=[
            pltpu.VMEM(activations.shape[1:], BF16),
            pltpu.VMEM(out_grads.shape[1:], BF16),
            pltpu.VMEM(proj_in.shape[1:], BF16),
            pltpu.VMEM(proj_out.shape[1:], BF16),
            pltpu.VMEM(queries.shape[1:], BF16),
            pltpu.SMEM((examples,), jnp.int32),
            pltpu.SMEM((examples,), jnp.int32),
            pltpu.VMEM((1, tok), jnp.int32),
            pltpu.VMEM((n_core - 1, part, r_out + r_in), F32),
            pltpu.VMEM((n_core - 1, part, r_out + r_in), F32),
            pltpu.VMEM((n_dp, part, r_out + r_in), BF16),
            pltpu.VMEM((r_out, part), F32),
            pltpu.VMEM((r_out * examples, 128), F32),
            pltpu.VMEM((examples, r_out * r_in), BF16),
            pltpu.VMEM((n_dp, rows, q_out), F32),
            pltpu.VMEM((sources, rows, q_out), F32),
            pltpu.SemaphoreType.DMA((32,)),
            pltpu.SemaphoreType.DMA((n_core - 1,)),
            pltpu.SemaphoreType.DMA((n_core - 1,)),
            pltpu.SemaphoreType.DMA((n_dp - 1,)),
            pltpu.SemaphoreType.DMA((n_dp - 1,)),
            pltpu.SemaphoreType.DMA((sources,)),
            pltpu.SemaphoreType.DMA((sources,)),
        ],
        compiler_params=pltpu.CompilerParams(
            collective_id=0, has_side_effects=True, vmem_limit_bytes=63 * 1024 * 1024
        ),
    )(
        activations, out_grads, proj_in, proj_out, queries, lengths, owner_slot,
        pad_mask.reshape(1, tok),
    )


def solution(mesh):
    sizes = (mesh.shape["dp"], mesh.shape["layer"], mesh.shape["tensor"])
    placed = (
        P("layer", ("groups", "dp"), "tensor"),
        P("layer", ("groups", "dp"), "tensor"),
        P("layer", None, "tensor"),
        P("layer", None, "tensor"),
        P("layer", "dp", None),
        P("groups"),
        P("groups"),
        P(("groups", "dp")),
    )
    return jax.shard_map(
        functools.partial(local, sizes), mesh=mesh, in_specs=placed,
        out_specs=P(("groups", "dp"), "layer"), check_vma=False,
    )
```
